256 devices in a mesh: row: 8 (over z_lo, x), col: 32 (over y, z_hi, core).
Axes of the slice: x: 4, y: 4, z: 8 (z_hi: 4, z_lo: 2; z = z_hi * 2 + z_lo), core: 2. Of those that a mesh axis runs over, the one named last changes fastest.
Arguments:
- tokens: bfloat16 [4096, 6144], P('row', 'col'), may hold values from -6 to 6
- weight: bfloat16 [6144, 24576], P('row', 'col'), may hold values from -0.078125 to 0.078125
- grad_out: bfloat16 [4096, 24576], P('row', 'col'), may hold values from -6 to 6
Outputs:
- activated: bfloat16 [4096, 24576], P('row', 'col')
- grad_tokens: bfloat16 [4096, 6144], P('row', 'col')
- grad_weight: bfloat16 [6144, 24576], P('row', 'col')
The draws below stay inside these ranges and needn't reach their ends.
All inputs are finite; a program needn't handle non-finite values.
Results may differ from the reference program's by a relative error of at most 0.025.
Values may be sent and summed in bfloat16 or wider, within the bound.
No kernel may reach another device: no remote copies, remote signals or barrier semaphores. Data moves between devices by JAX's collectives and lax.ppermute only.
A program may use at most 128 MiB of HBM per device.

```python
import math
import jax
import jax.numpy as jnp
from jax import lax

D = 6144
FF = 24576
TOK_DEV = 512
TOKENS = 4096
N_ROW = 8
N_COL = 32


def block_scale(stream_key, dims, split, smallest, high):
    gain, own = 1.0, jax.random.fold_in(stream_key, 6)
    for dim, parts in split:
        heights = jnp.exp(jax.random.uniform(jax.random.fold_in(own, dim), (parts,), jnp.float32, smallest / len(split), high / len(split)))
        gain = gain * jnp.repeat(heights, dims[dim] // parts).reshape([-1 if axis == dim else 1 for axis in range(len(dims))])
    return gain


def gaussian(rng, shape, spread, reach, cuts=(), dtype=jnp.bfloat16):
    entries = jax.random.normal(rng, shape, jnp.float32) * spread
    if len(cuts) > 0:
        entries = block_scale(rng, shape, cuts, -0.22, 0.18) * entries
    return jnp.clip(entries, min=-reach, max=reach).astype(dtype)


def setup_inputs(seed: int = 0) -> dict:
    key_of = jax.random.split(jax.random.key(seed), 4)
    return {
        "tokens": gaussian(key_of[0], (TOKENS, D), 1.0, 6.0, ((0, 8), (1, 32))),
        "weight": gaussian(key_of[1], (D, FF), D ** -0.5, 0.078125, ((0, 8), (1, 32))),
        "grad_out": gaussian(key_of[2], (TOKENS, FF), 1.0, 6.0, ((0, 8), (1, 32))),
    }


slope_coef = math.sqrt(2.0 / math.pi)

def gelu_value(values):
    inside_arg = slope_coef * (values + 0.044715 * values * values * values)
    return 0.5 * values * (1.0 + jnp.tanh(inside_arg))

def gelu_slope(values):
    inside_arg = slope_coef * (values + 0.044715 * values * values * values)
    tangent = jnp.tanh(inside_arg)
    return 0.5 * (1.0 + tangent) + 0.5 * values * (1.0 - tangent * tangent) * slope_coef * (1.0 + 3.0 * 0.044715 * values * values)

def rounded(values):
    return lax.optimization_barrier(values.astype(jnp.bfloat16)).astype(jnp.float32)

def reference(tokens, weight, grad_out):
    pre_act = jnp.dot(tokens, weight, preferred_element_type=jnp.float32)
    activated = gelu_value(pre_act).astype(jnp.bfloat16)
    grad_pre = (grad_out.astype(jnp.float32) * gelu_slope(pre_act)).astype(jnp.bfloat16)
    ff_block = FF // N_COL
    grad_blocks = grad_pre.reshape(TOKENS, N_COL, ff_block).transpose(1, 0, 2)
    weight_blocks = weight.reshape(D, N_COL, ff_block).transpose(1, 0, 2)

    def add_input(running, pair):
        partial_sum = jnp.dot(pair[0], pair[1].T, preferred_element_type=jnp.float32)
        return (running + rounded(partial_sum), None)
    grad_tokens, _ = lax.scan(add_input, jnp.zeros((TOKENS, D), jnp.float32), (grad_blocks, weight_blocks))
    token_blocks = tokens.reshape(N_ROW, TOK_DEV, D)
    grad_rows = grad_pre.reshape(N_ROW, TOK_DEV, FF)

    def add_weight(running, pair):
        partial_sum = jnp.dot(pair[0].T, pair[1], preferred_element_type=jnp.float32)
        return (running + rounded(partial_sum), None)
    grad_weight, _ = lax.scan(add_weight, jnp.zeros((D, FF), jnp.float32), (token_blocks, grad_rows))
    return (activated, grad_tokens.astype(jnp.bfloat16), grad_weight.astype(jnp.bfloat16))
```

```python
import functools
import math

import jax
import jax.numpy as jnp
from jax import lax
from jax.experimental import pallas as pl
from jax.experimental.pallas import tpu as pltpu
from jax.sharding import Mesh
from jax.sharding import PartitionSpec as P

slope_coef = math.sqrt(2.0 / math.pi)
AXES = ("zl", "x", "y", "zh", "c")
CHUNKS = ((0, 256), (256, 256))
BF16, F32 = jnp.bfloat16, jnp.float32
VMEM_LIMIT = 44 * 1024 * 1024


def flip(value, axis, mask):
    size = {"zl": 2, "x": 4, "y": 4, "zh": 4, "c": 2}[axis]
    return lax.ppermute(value, axis, [(i, i ^ mask) for i in range(size)])


def spread_pairs():
    pairs = []
    for x in range(4):
        for y in range(4):
            for zh in range(4):
                to_x = (y % 2) * 2 + zh // 2
                to_y = (y // 2) * 2 + x // 2
                to_zh = (x % 2) * 2 + zh % 2
                pairs.append(((x * 4 + y) * 4 + zh, (to_x * 4 + to_y) * 4 + to_zh))
    return pairs


def project_kernel(idx, *refs):
    stacks, (w_own, w_other), (p0, p1, p2, p3, a_out) = refs[:8], refs[8:10], refs[10:15]
    a_v, w_v, sems, out_sem = refs[15:]
    zl, x, y, zh, c = (idx[i] for i in range(5))
    copies = []
    for dc in range(2):
        for dy in range(4):
            for dz in range(4):
                ny, nz = y ^ dy, zh ^ dz
                block = x ^ ((ny & 1) * 2 + (nz >> 1))
                row = pl.multiple_of((ny >> 1) * 768 + ((nz & 1) * 2 + (c ^ dc)) * 192, 64)
                copies.append(
                    pltpu.make_async_copy(
                        stacks[dc * 4 + dy].at[dz],
                        a_v.at[block, pl.ds(row, 192), :],
                        sems.at[len(copies)],
                    )
                )
    for ref, half in ((w_own, zl), (w_other, zl ^ 1)):
        row = pl.multiple_of(half * 768, 768)
        copies.append(
            pltpu.make_async_copy(ref, w_v.at[pl.ds(row, 768), :], sems.at[len(copies)])
        )
    for copy in copies:
        copy.start()
    for copy in copies:
        copy.wait()
    back = pltpu.make_async_copy(a_v, a_out, out_sem)
    back.start()
    for block, out in ((1, p1), (2, p2), (3, p3), (0, p0)):
        out[...] = lax.dot_general(
            a_v[block], w_v[...], (((0,), (0,)), ((), ())), preferred_element_type=F32
        ).astype(out.dtype)
    back.wait()


def project(idx, stacks, w_own, w_other, width):
    hbm = pl.BlockSpec(memory_space=pl.ANY)
    vmem = pl.BlockSpec(memory_space=pltpu.VMEM)
    out = [jax.ShapeDtypeStruct((width, 768), F32)]
    out += [jax.ShapeDtypeStruct((width, 768), BF16)] * 3
    out += [jax.ShapeDtypeStruct((4, 1536, width), BF16)]
    return pl.pallas_call(
        project_kernel,
        out_shape=out,
        in_specs=[pl.BlockSpec(memory_space=pltpu.SMEM)] + [hbm] * 10,
        out_specs=[vmem] * 4 + [hbm],
        scratch_shapes=[
            pltpu.VMEM((4, 1536, width), BF16),
            pltpu.VMEM((1536, 768), BF16),
            pltpu.SemaphoreType.DMA((34,)),
            pltpu.SemaphoreType.DMA,
        ],
        compiler_params=pltpu.CompilerParams(vmem_limit_bytes=VMEM_LIMIT),
        cost_estimate=pl.CostEstimate(
            flops=2 * 4 * width * 1536 * 768, bytes_accessed=30 * 1024 * width, transcendentals=0
        ),
    )(idx, *stacks, w_own, w_other)


def input_grad_kernel(idx, g0, g1, g2, g3, w_own, w_other, keep, send):
    zl, x, y, zh, c = (idx[i] for i in range(5))
    first = c == 0
    for rel, g in ((0, g0), (1, g1), (2, g2), (3, g3)):
        block = x ^ rel
        for w, half in ((w_own, zl), (w_other, zl ^ 1)):
            part = lax.dot_general(
                w[...], g[...], (((1,), (1,)), ((), ())), preferred_element_type=F32
            )
            dy = y ^ (half * 2 + (block >> 1))
            for high in range(2):
                even = part[high * 384 : high * 384 + 192, :]
                odd = part[high * 384 + 192 : high * 384 + 384, :]
                dz = zh ^ ((block & 1) * 2 + high)
                keep[dy * 4 + dz] = jnp.where(first, even, odd).astype(BF16)
                send[dy * 4 + dz] = jnp.where(first, odd, even).astype(BF16)


def input_grad(idx, grads, w_own, w_other, width):
    vmem = pl.BlockSpec(memory_space=pltpu.VMEM)
    return pl.pallas_call(
        input_grad_kernel,
        out_shape=[jax.ShapeDtypeStruct((16, 192, width), BF16)] * 2,
        in_specs=[pl.BlockSpec(memory_space=pltpu.SMEM)] + [vmem] * 6,
        out_specs=[vmem] * 2,
        compiler_params=pltpu.CompilerParams(vmem_limit_bytes=VMEM_LIMIT),
        cost_estimate=pl.CostEstimate(
            flops=2 * 4 * width * 1536 * 768, bytes_accessed=30 * 1024 * width, transcendentals=0
        ),
    )(idx, *grads, w_own, w_other)


def weight_grad_kernel(flipped, count, idx, *refs):
    grads, gathered, (out,) = refs[: 4 * count], refs[4 * count : 5 * count], refs[5 * count : 5 * count + 1]
    a_vs, sems = refs[5 * count + 1 : -1], refs[-1]
    row = pl.multiple_of((idx[0] ^ flipped) * 768, 768)
    copies = [
        pltpu.make_async_copy(a.at[:, pl.ds(row, 768), :], a_v, sems.at[i])
        for i, (a, a_v) in enumerate(zip(gathered, a_vs))
    ]
    for copy in copies:
        copy.start()
    total = None
    for i, (copy, a_v) in enumerate(zip(copies, a_vs)):
        copy.wait()
        for block in range(4):
            term = jnp.dot(a_v[block], grads[4 * i + block][...], preferred_element_type=F32)
            total = term if total is None else total + term
    out[...] = total.astype(out.dtype)


def weight_grad(idx, grads, gathered, flipped, dtype):
    count = len(gathered)
    vmem = pl.BlockSpec(memory_space=pltpu.VMEM)
    hbm = pl.BlockSpec(memory_space=pl.ANY)
    return pl.pallas_call(
        functools.partial(weight_grad_kernel, flipped, count),
        out_shape=jax.ShapeDtypeStruct((768, 768), dtype),
        in_specs=[pl.BlockSpec(memory_space=pltpu.SMEM)] + [vmem] * (4 * count) + [hbm] * count,
        out_specs=vmem,
        scratch_shapes=[pltpu.VMEM((4, 768, a.shape[2]), BF16) for a in gathered]
        + [pltpu.SemaphoreType.DMA((count,))],
        compiler_params=pltpu.CompilerParams(vmem_limit_bytes=VMEM_LIMIT),
        cost_estimate=pl.CostEstimate(
            flops=2 * 2048 * 768 * 768, bytes_accessed=8 * 1024 * 1024, transcendentals=0
        ),
    )(idx, *[g for chunk in grads for g in chunk], *gathered)


def gelu_pair(pre_act, grad_out):
    inside = slope_coef * (pre_act + 0.044715 * pre_act * pre_act * pre_act)
    tangent = jnp.tanh(inside)
    activated = 0.5 * pre_act * (1.0 + tangent)
    slope = 0.5 * (1.0 + tangent) + 0.5 * pre_act * (1.0 - tangent * tangent) * slope_coef * (
        1.0 + 3.0 * 0.044715 * pre_act * pre_act
    )
    return activated.astype(BF16), (grad_out.astype(F32) * slope).astype(BF16)


def per_device(tokens, weight, grad_out):
    idx = jnp.stack([lax.axis_index(axis) for axis in AXES]).astype(jnp.int32)
    pairs = spread_pairs()
    spread = lax.ppermute(tokens.T, ("x", "y", "zh"), pairs)
    w_other = flip(weight, "zl", 1)

    gathered, partials = [], []
    for start, width in CHUNKS:
        piece = spread[:, start : start + width]
        line = jnp.stack([piece] + [flip(piece, "zh", d) for d in (1, 2, 3)])
        planes = [line] + [flip(line, "y", d) for d in (1, 2, 3)]
        stacks = planes + [flip(plane, "c", 1) for plane in planes]
        *parts, a_all = project(idx, stacks, weight, w_other, width)
        partials.append(parts)
        gathered.append(a_all)

    activated, grads = [], []
    for (start, width), parts in zip(CHUNKS, partials):
        pre_act = parts[0]
        for d in (1, 2, 3):
            pre_act = pre_act + flip(parts[d], "x", d).astype(F32)
        act, grad_pre = gelu_pair(pre_act, grad_out[start : start + width])
        activated.append(act)
        grads.append([grad_pre] + [flip(grad_pre, "x", d) for d in (1, 2, 3)])

    final = []
    for (start, width), grad in zip(CHUNKS, grads):
        keep, send = input_grad(idx, grad, weight, w_other, width)
        both = keep.astype(F32) + flip(send, "c", 1).astype(F32)
        both = both.astype(BF16).reshape(4, 4, 192, width)
        line = both[0].astype(F32)
        for d in (1, 2, 3):
            line = line + flip(both[d], "y", d).astype(F32)
        line = line.astype(BF16)
        piece = line[0].astype(F32)
        for d in (1, 2, 3):
            piece = piece + flip(line[d], "zh", d).astype(F32)
        final.append(piece.astype(BF16))
    grad_tokens = lax.ppermute(
        jnp.concatenate(final, axis=1), ("x", "y", "zh"), [(b, a) for a, b in pairs]
    ).T

    theirs = weight_grad(idx, grads, gathered, 1, BF16)
    mine = weight_grad(idx, grads, gathered, 0, F32)
    grad_weight = (mine + flip(theirs, "zl", 1).astype(F32)).astype(BF16)
    return jnp.concatenate(activated, axis=0), grad_tokens, grad_weight


def solution(mesh):
    fine = Mesh(mesh.devices.reshape(2, 4, 4, 4, 2), AXES)
    spec = P(("zl", "x"), ("y", "zh", "c"))
    return jax.shard_map(
        per_device, mesh=fine, in_specs=(spec,) * 3, out_specs=(spec,) * 3, check_vma=False
    )
```

```python
import functools
import math

import jax
import jax.numpy as jnp
from jax import lax
from jax.experimental import pallas as pl
from jax.experimental.pallas import tpu as pltpu
from jax.sharding import Mesh
from jax.sharding import PartitionSpec as P

slope_coef = math.sqrt(2.0 / math.pi)
AXES = ("zl", "x", "y", "zh", "c")
SIZES = {"zl": 2, "x": 4, "y": 4, "zh": 4, "c": 2}
BF16, F32 = jnp.bfloat16, jnp.float32
VMEM_LIMIT = 40 * 1024 * 1024
HBM = pl.BlockSpec(memory_space=pl.ANY)
VMEM = pl.BlockSpec(memory_space=pltpu.VMEM)
SMEM = pl.BlockSpec(memory_space=pltpu.SMEM)


def flip(value, axis, mask):
    return lax.ppermute(value, axis, [(i, i ^ mask) for i in range(SIZES[axis])])


def over_z(value):
    return flip(value, "zl", 1)


def spread_pairs():
    pairs = []
    for zl in range(2):
        for y in range(4):
            to_y = y if y >> 1 == zl else y ^ 3
            pairs.append((zl * 4 + y, (y >> 1) * 4 + to_y))
    return pairs


def spread(value):
    return lax.ppermute(value, ("zl", "y"), spread_pairs())


def spread_back(value):
    return lax.ppermute(value, ("zl", "y"), [(b, a) for a, b in spread_pairs()])


def call(kernel, out_shape, in_specs, out_specs, scratch, flops, nbytes):
    return pl.pallas_call(
        kernel,
        out_shape=out_shape,
        in_specs=in_specs,
        out_specs=out_specs,
        scratch_shapes=scratch,
        compiler_params=pltpu.CompilerParams(vmem_limit_bytes=VMEM_LIMIT),
        cost_estimate=pl.CostEstimate(flops=flops, bytes_accessed=nbytes, transcendentals=0),
    )


def run_copies(copies):
    for copy in copies:
        copy.start()
    for copy in copies:
        copy.wait()


def weight_row(idx, near, dz, dc):
    zl, y, zh, c = idx[0], idx[2], idx[3], idx[4]
    upper = near ^ zl ^ (y & 1) ^ (y >> 1)
    return pl.multiple_of(((upper * 4 + (zh ^ dz)) * 2 + (c ^ dc)) * 192, 192)


def arrange_kernel(idx, w, out, sems):
    copies = []
    for dc in range(2):
        for near in range(2):
            for dz in range(4):
                copies.append(
                    pltpu.make_async_copy(
                        w.at[pl.ds(weight_row(idx, near, dz, dc), 192), :],
                        out.at[dc, pl.ds((near * 4 + dz) * 192, 192), :],
                        sems.at[len(copies)],
                    )
                )
    run_copies(copies)


def arrange(idx, w):
    return call(
        arrange_kernel,
        jax.ShapeDtypeStruct((2, 1536, 768), BF16),
        [SMEM, HBM],
        HBM,
        [pltpu.SemaphoreType.DMA((16,))],
        0,
        10 << 20,
    )(idx, w)


def join_kernel(n, *refs):
    *ins, out, sems = refs
    copies = []
    for i, a in enumerate(ins):
        copies.append(pltpu.make_async_copy(a, out.at[pl.ds(i * n, n), :], sems.at[i]))
    run_copies(copies)


def join(*values):
    rows, width = values[0].shape
    return call(
        functools.partial(join_kernel, rows),
        jax.ShapeDtypeStruct((len(values) * rows, width), BF16),
        [HBM] * len(values),
        HBM,
        [pltpu.SemaphoreType.DMA((len(values),))],
        0,
        4 * len(values) * rows * width,
    )(*values)


def across(a, w):
    return lax.dot_general(a, w, (((0,), (0,)), ((), ())), preferred_element_type=F32)


def turn_of(idx):
    return idx[0] ^ (idx[2] >> 1)


def first_kernel(idx, a, w, out):
    for rel in range(2):
        out[rel] = across(a[rel ^ turn_of(idx)], w[0])


def second_kernel(idx, acc, a, w, mine, theirs):
    for rel, out in ((1, theirs), (0, mine)):
        out[...] = (acc[rel] + across(a[rel ^ turn_of(idx)], w[1])).astype(out.dtype)


def project_first(idx, a_own, w_rel, width):
    return call(
        first_kernel,
        jax.ShapeDtypeStruct((2, width, 768), F32),
        [SMEM, VMEM, VMEM],
        VMEM,
        [],
        8 * width * 768 * 768,
        20 * 1024 * width,
    )(idx, a_own.reshape(2, 1536, width), w_rel)


def project_second(idx, acc, a_other, w_rel, width):
    return call(
        second_kernel,
        [jax.ShapeDtypeStruct((width, 768), F32), jax.ShapeDtypeStruct((width, 768), BF16)],
        [SMEM, VMEM, VMEM, VMEM],
        [VMEM] * 2,
        [],
        8 * width * 768 * 768,
        20 * 1024 * width,
    )(idx, acc, a_other.reshape(2, 1536, width), w_rel)


def input_grad_kernel(which, idx, g0, g1, w, out):
    for rel, g in enumerate((g0, g1)):
        block = rel ^ turn_of(idx)
        part = lax.dot_general(
            w[which], g[...], (((1,), (1,)), ((), ())), preferred_element_type=F32
        ).astype(BF16)
        for near in range(2):
            out[block * 2 + (near ^ block)] = part[near * 768 : near * 768 + 768]


def input_grad(idx, grads, w_rel, which, width):
    return call(
        functools.partial(input_grad_kernel, which),
        jax.ShapeDtypeStruct((4, 768, width), BF16),
        [SMEM] + [VMEM] * 3,
        VMEM,
        [],
        8 * width * 768 * 768,
        20 * 1024 * width,
    )(idx, *grads, w_rel)


def weight_grad_kernel(count, idx, *refs):
    grads, gathered, out = refs[: 2 * count], refs[2 * count : 4 * count], refs[4 * count]
    for dc in range(2):
        for near in range(2):
            total = None
            for i in range(count):
                a = gathered[2 * i + dc]
                for rel in range(2):
                    term = jnp.dot(
                        a[rel ^ turn_of(idx), near * 768 : near * 768 + 768, :],
                        grads[2 * i + rel][...],
                        preferred_element_type=F32,
                    )
                    total = term if total is None else total + term
            total = total.astype(BF16)
            for dz in range(4):
                out[pl.ds(weight_row(idx, near, dz, dc), 192), :] = total[dz * 192 : dz * 192 + 192]


def weight_grad(idx, grads, gathered):
    count = len(grads) // 2
    width = grads[0].shape[0]
    return call(
        functools.partial(weight_grad_kernel, count),
        jax.ShapeDtypeStruct((3072, 768), BF16),
        [SMEM] + [VMEM] * (4 * count),
        VMEM,
        [],
        8 * count * width * 1536 * 768,
        16 << 20,
    )(idx, *grads, *[a.reshape(2, 1536, width) for a in gathered])


def gelu_pair(pre_act, grad_out):
    inside = slope_coef * (pre_act + 0.044715 * pre_act * pre_act * pre_act)
    tangent = jnp.tanh(inside)
    activated = 0.5 * pre_act * (1.0 + tangent)
    slope = 0.5 * (1.0 + tangent) + 0.5 * pre_act * (1.0 - tangent * tangent) * slope_coef * (
        1.0 + 3.0 * 0.044715 * pre_act * pre_act
    )
    return activated.astype(BF16), (grad_out.astype(F32) * slope).astype(BF16)


def stage(*values):
    return lax.optimization_barrier(values)


def added(first, others):
    total = first.astype(F32)
    for other in others:
        total = total + other.astype(F32)
    return total


def gather_pieces(value, axis):
    return [value] + [flip(value, axis, d) for d in (1, 2, 3)]


def in_order(planes):
    return join(planes[0], planes[1], planes[3], planes[2])


def per_device(tokens, weight, grad_out):
    idx = jnp.stack([lax.axis_index(axis) for axis in AXES]).astype(jnp.int32)
    n = 256
    w_all = lax.all_gather(weight, "x", axis=0, tiled=True)
    w_rel = arrange(idx, w_all)
    piece = spread(tokens.T)
    piece_a, piece_b = piece[:, :n], piece[:, n:]
    *pieces_a, piece_b = stage(*gather_pieces(piece_a, "zh"), piece_b)

    pieces_b = gather_pieces(piece_b, "zh")
    planes_a = gather_pieces(join(*pieces_a), "y")
    stages = stage(*planes_a, *pieces_b)
    planes_a, pieces_b = stages[:4], stages[4:]

    own_a = in_order(planes_a)
    planes_b = gather_pieces(join(*pieces_b), "y")
    other_a = flip(own_a, "c", 1)
    acc = project_first(idx, own_a, w_rel, n)
    p_a, send = project_second(idx, acc, other_a, w_rel, n)
    *planes_b, came_a = stage(*planes_b, over_z(send))

    own_b = in_order(planes_b)
    act_a, grad_a = gelu_pair(added(p_a, [came_a]), grad_out[:n])
    other_b = flip(own_b, "c", 1)
    acc = project_first(idx, own_b, w_rel, n)
    p_b, send = project_second(idx, acc, other_b, w_rel, n)
    grad_a2, send = stage(over_z(grad_a), send)

    all_a = [grad_a, grad_a2]
    came_b = over_z(send)
    half = flip(input_grad(idx, all_a, w_rel, 1, n), "c", 1)
    both_a = added(input_grad(idx, all_a, w_rel, 0, n), [half]).astype(BF16)
    came_b, both_a = stage(came_b, both_a)

    act_b, grad_b = gelu_pair(added(p_b, [came_b]), grad_out[n:])
    grad_b2, *rows_a = stage(over_z(grad_b), *[flip(both_a[d], "y", d) for d in (1, 2, 3)])

    all_b = [grad_b, grad_b2]
    half = flip(input_grad(idx, all_b, w_rel, 1, n), "c", 1)
    partial = weight_grad(idx, all_a + all_b, [own_a, other_a, own_b, other_b])
    grad_weight = lax.psum_scatter(partial, "x", scatter_dimension=0, tiled=True)
    both_b = added(input_grad(idx, all_b, w_rel, 0, n), [half]).astype(BF16)
    line_a = added(both_a[0], rows_a).astype(BF16).reshape(4, 192, n)
    both_b, line_a = stage(both_b, line_a)

    rows_b = [flip(both_b[d], "y", d) for d in (1, 2, 3)]
    homes_a = [flip(line_a[d], "zh", d) for d in (1, 2, 3)]
    stages = stage(*rows_b, *homes_a)
    rows_b, homes_a = stages[:3], stages[3:]

    line_b = added(both_b[0], rows_b).astype(BF16).reshape(4, 192, n)
    homes_b = [flip(line_b[d], "zh", d) for d in (1, 2, 3)]
    final_a = spread_back(added(line_a[0], homes_a).astype(BF16))
    *homes_b, final_a = stage(*homes_b, final_a)
    final_b = spread_back(added(line_b[0], homes_b).astype(BF16))
    grad_tokens = jnp.concatenate([final_a, final_b], axis=1).T
    return jnp.concatenate([act_a, act_b], axis=0), grad_tokens, grad_weight


def solution(mesh):
    fine = Mesh(mesh.devices.reshape(2, 4, 4, 4, 2), AXES)
    spec = P(("zl", "x"), ("y", "zh", "c"))
    return jax.shard_map(
        per_device, mesh=fine, in_specs=(spec,) * 3, out_specs=(spec,) * 3, check_vma=False
    )
```

```python
import functools
import math

import jax
import jax.numpy as jnp
from jax import lax
from jax.experimental import pallas as pl
from jax.experimental.pallas import tpu as pltpu
from jax.sharding import Mesh
from jax.sharding import PartitionSpec as P

slope_coef = math.sqrt(2.0 / math.pi)
AXES = ("zl", "x", "y", "zh", "c")
SIZES = {"zl": 2, "x": 4, "y": 4, "zh": 4, "c": 2}
BF16, F32 = jnp.bfloat16, jnp.float32
MIB = 1024 * 1024
HBM = pl.BlockSpec(memory_space=pl.ANY)
VMEM = pl.BlockSpec(memory_space=pltpu.VMEM)
SMEM = pl.BlockSpec(memory_space=pltpu.SMEM)


def flip(value, axis, mask):
    return lax.ppermute(value, axis, [(i, i ^ mask) for i in range(SIZES[axis])])


def over_z(value):
    return flip(value, "zl", 1)


def over_near(value):
    return flip(value, "y", 1)


def over_far(value):
    return flip(value, "y", 3)


def add_top(block, came):
    n = came.shape[0]
    return jnp.concatenate([added(block[:n], [came]).astype(BF16), block[n:]])


def add_low(block, came):
    n = block.shape[0] - came.shape[0]
    return jnp.concatenate([block[:n], added(block[n:], [came]).astype(BF16)])


def spread_pairs(turn):
    pairs = []
    for zl in range(2):
        for y in range(4):
            to_y = y if y >> 1 == zl ^ turn else y ^ 3
            pairs.append((zl * 4 + y, (y >> 1) * 4 + to_y))
    return pairs


def spread(value, turn):
    return lax.ppermute(value, ("zl", "y"), spread_pairs(turn))


def spread_back(value, turn):
    return lax.ppermute(value, ("zl", "y"), [(b, a) for a, b in spread_pairs(turn)])


def call(kernel, out_shape, in_specs, out_specs, scratch, flops, nbytes, limit):
    return pl.pallas_call(
        kernel,
        out_shape=out_shape,
        in_specs=in_specs,
        out_specs=out_specs,
        scratch_shapes=scratch,
        compiler_params=pltpu.CompilerParams(vmem_limit_bytes=limit),
        cost_estimate=pl.CostEstimate(flops=flops, bytes_accessed=nbytes, transcendentals=0),
    )


def run_copies(copies):
    for copy in copies:
        copy.start()
    for copy in copies:
        copy.wait()


def weight_row(idx, near, dz, dc):
    zl, y, zh, c = idx[0], idx[2], idx[3], idx[4]
    upper = near ^ zl ^ (y & 1) ^ (y >> 1)
    return pl.multiple_of(((upper * 4 + (zh ^ dz)) * 2 + (c ^ dc)) * 192, 192)


def join_kernel(n, *refs):
    *ins, out, sems = refs
    copies = []
    for i, a in enumerate(ins):
        copies.append(pltpu.make_async_copy(a, out.at[pl.ds(i * n, n), :], sems.at[i]))
    run_copies(copies)


def join(*values):
    rows, width = values[0].shape
    return call(
        functools.partial(join_kernel, rows),
        jax.ShapeDtypeStruct((len(values) * rows, width), BF16),
        [HBM] * len(values),
        VMEM,
        [pltpu.SemaphoreType.DMA((len(values),))],
        0,
        4 * len(values) * rows * width,
        8 * MIB,
    )(*values)


def across(a, w):
    return lax.dot_general(a, w, (((0,), (0,)), ((), ())), preferred_element_type=F32)


def turn_of(idx):
    return idx[2] >> 1


def project_kernel(idx, own, other, w, out, w0, w1, a_v, w_v, acc, a_sems, w_sems, out_sems):
    loads = [
        pltpu.make_async_copy(a, a_v.at[dc], a_sems.at[dc]) for dc, a in enumerate((own, other))
    ]
    copies = []
    for dc in range(2):
        for near in range(2):
            for dz in range(4):
                copies.append(
                    pltpu.make_async_copy(
                        w.at[pl.ds(weight_row(idx, near, dz, dc), 192), :],
                        w_v.at[dc, pl.ds((near * 4 + dz) * 192, 192), :],
                        w_sems.at[len(copies)],
                    )
                )
    loads[0].start()
    for copy in copies[:8]:
        copy.start()
    loads[1].start()
    for copy in copies[8:]:
        copy.start()
    stores = []
    n = a_v.shape[-1]
    for step in range(4):
        dc, near = step // 2, step % 2
        if near == 0:
            loads[dc].wait()
        for copy in copies[4 * step : 4 * step + 4]:
            copy.wait()
        if near == 1:
            stores.append(pltpu.make_async_copy(w_v.at[dc], (w0, w1)[dc], out_sems.at[dc]))
            stores[-1].start()
        rows = slice(near * 768, near * 768 + 768)
        for half in range(2):
            part = across(a_v[dc, half ^ turn_of(idx), rows], w_v[dc, rows])
            if step > 0:
                part = acc[half] + part
            if step < 3:
                acc[half] = part
            else:
                out[half * n : half * n + n] = part.astype(BF16)
    for store in stores:
        store.wait()


def project(idx, own, other, w_all):
    width = own.shape[-1]
    return call(
        project_kernel,
        [jax.ShapeDtypeStruct((2 * width, 768), BF16)]
        + [jax.ShapeDtypeStruct((1536, 768), BF16)] * 2,
        [SMEM, HBM, HBM, HBM],
        [VMEM, HBM, HBM],
        [
            pltpu.VMEM((2, 2, 1536, width), BF16),
            pltpu.VMEM((2, 1536, 768), BF16),
            pltpu.VMEM((2, width, 768), F32),
            pltpu.SemaphoreType.DMA((2,)),
            pltpu.SemaphoreType.DMA((16,)),
            pltpu.SemaphoreType.DMA((2,)),
        ],
        16 * width * 768 * 768,
        20 << 20,
        58 * MIB,
    )(idx, own.reshape(2, 1536, width), other.reshape(2, 1536, width), w_all)


def half_kernel(idx, a, w, *refs):
    *acc, out = refs
    n = a.shape[-1]
    for half in range(2):
        rows = slice(half * n, half * n + n)
        part = across(a[half ^ turn_of(idx)], w[...])
        out[rows] = acc[0][rows] + part if acc else part


def project_half(idx, a, w, acc):
    width = a.shape[-1]
    return call(
        half_kernel,
        jax.ShapeDtypeStruct((2 * width, 768), F32),
        [SMEM] + [VMEM] * (2 + len(acc)),
        VMEM,
        [],
        8 * width * 768 * 768,
        20 * 1024 * width,
        20 * MIB,
    )(idx, a.reshape(2, 1536, width), w, *acc)


def input_grad_kernel(idx, g, w, out):
    n = out.shape[-1]
    for half in range(2):
        upper = half ^ turn_of(idx)
        part = lax.dot_general(
            w[...],
            g[half * n : half * n + n],
            (((1,), (1,)), ((), ())),
            preferred_element_type=F32,
        ).astype(BF16)
        for near in range(2):
            out[upper * 2 + (near ^ upper)] = part[near * 768 : near * 768 + 768]


def input_grad(idx, g, w):
    width = g.shape[0] // 2
    return call(
        input_grad_kernel,
        jax.ShapeDtypeStruct((4, 768, width), BF16),
        [SMEM] + [VMEM] * 2,
        VMEM,
        [],
        8 * width * 768 * 768,
        20 * 1024 * width,
        20 * MIB,
    )(idx, g, w)


def weight_grad_kernel(idx, g, own, other, *refs):
    *acc, out = refs
    n = own.shape[-1]
    for dc, a in enumerate((own, other)):
        for near in range(2):
            total = None
            for half in range(2):
                term = jnp.dot(
                    a[half ^ turn_of(idx), near * 768 : near * 768 + 768, :],
                    g[half * n : half * n + n],
                    preferred_element_type=F32,
                )
                total = term if total is None else total + term
            for dz in range(4):
                part = total[dz * 192 : dz * 192 + 192]
                rows = pl.ds(weight_row(idx, near, dz, dc), 192)
                if acc:
                    part = part + acc[0][rows, :].astype(F32)
                out[rows, :] = part.astype(BF16)


def weight_grad(idx, g, own, other, acc):
    width = own.shape[-1]
    return call(
        weight_grad_kernel,
        jax.ShapeDtypeStruct((3072, 768), BF16),
        [SMEM] + [VMEM] * (3 + len(acc)),
        VMEM,
        [],
        16 * width * 768 * 768,
        16 << 20,
        24 * MIB,
    )(idx, g, own.reshape(2, 1536, width), other.reshape(2, 1536, width), *acc)


def gelu_pair(pre_act, grad_out):
    inside = slope_coef * (pre_act + 0.044715 * pre_act * pre_act * pre_act)
    tangent = jnp.tanh(inside)
    activated = 0.5 * pre_act * (1.0 + tangent)
    slope = 0.5 * (1.0 + tangent) + 0.5 * pre_act * (1.0 - tangent * tangent) * slope_coef * (
        1.0 + 3.0 * 0.044715 * pre_act * pre_act
    )
    return activated.astype(BF16), (grad_out.astype(F32) * slope).astype(BF16)


def stage(*values):
    return lax.optimization_barrier(values)


def added(first, others):
    total = first.astype(F32)
    for other in others:
        total = total + other.astype(F32)
    return total


def gather_pieces(value, axis):
    return [value] + [flip(value, axis, d) for d in (1, 2, 3)]


def in_order(planes):
    return join(planes[0], planes[1], planes[3], planes[2])


def per_device(tokens, weight, grad_out):
    idx = jnp.stack([lax.axis_index(axis) for axis in AXES]).astype(jnp.int32)
    n = 256
    w_all = lax.all_gather(weight, "x", axis=0, tiled=True)
    zl, upper = idx[0], idx[2] >> 1
    turned = tokens.T
    first, last = turned[:, :n], turned[:, n:]
    came0 = spread(jnp.where(zl == 0, first, last), 0)
    came1 = spread(jnp.where(zl == 0, last, first), 1)
    piece_p = jnp.where(upper == zl, came1, came0)
    piece_o = jnp.where(upper == zl, came0, came1)
    *pieces_p, piece_o = stage(*gather_pieces(piece_p, "zh"), piece_o)

    pieces_o = gather_pieces(piece_o, "zh")
    planes_p = gather_pieces(join(*pieces_p), "y")
    stages = stage(*planes_p, *pieces_o)
    planes_p, pieces_o = stages[:4], stages[4:]

    own_p = in_order(planes_p)
    planes_o = gather_pieces(join(*pieces_o), "y")
    other_p = flip(own_p, "c", 1)
    send, w0, w1 = project(idx, own_p, other_p, w_all)
    came = over_z(send)
    *planes_o, w0 = stage(*planes_o, w0)

    own_o = in_order(planes_o)
    other_o = flip(own_o, "c", 1)
    pre_act = project_half(idx, other_o, w1, [project_half(idx, own_o, w0, [])])
    activated, grad_o = gelu_pair(added(pre_act, [came]), grad_out)
    grad_p = over_z(grad_o)

    half = flip(input_grad(idx, grad_o, w1), "c", 1)
    both_o = added(input_grad(idx, grad_o, w0), [half]).astype(BF16)
    rows_o = [flip(both_o[d], "y", d) for d in (1, 2, 3)]
    partial = weight_grad(idx, grad_o, own_o, other_o, [])
    grad_p, partial, *rows_o = stage(grad_p, partial, *rows_o)

    partial = weight_grad(idx, grad_p, own_p, other_p, [partial])
    partial, grad_p = stage(partial, grad_p)
    grad_weight = lax.psum_scatter(partial, "x", scatter_dimension=0, tiled=True)
    half = flip(input_grad(idx, grad_p, w1), "c", 1)
    both_p = added(input_grad(idx, grad_p, w0), [half]).astype(BF16)
    rows_p = [flip(both_p[d], "y", d) for d in (1, 2, 3)]
    line_o = added(both_o[0], rows_o).astype(BF16).reshape(4, 192, n)
    homes_o = [flip(line_o[d], "zh", d) for d in (1, 2, 3)]
    stages = stage(*rows_p, *homes_o)
    rows_p, homes_o = stages[:3], stages[3:]
    line_p = added(both_p[0], rows_p).astype(BF16).reshape(4, 192, n)
    homes_p = [flip(line_p[d], "zh", d) for d in (1, 2, 3)]
    final_o = added(line_o[0], homes_o).astype(BF16)
    final_p = added(line_p[0], homes_p).astype(BF16)
    back0 = spread_back(jnp.where(upper == zl, final_o, final_p), 0)
    back1 = spread_back(jnp.where(upper == zl, final_p, final_o), 1)
    first = jnp.where(zl == 0, back0, back1)
    last = jnp.where(zl == 0, back1, back0)
    grad_tokens = jnp.concatenate([first, last], axis=1).T
    return activated, grad_tokens, grad_weight


def solution(mesh):
    fine = Mesh(mesh.devices.reshape(2, 4, 4, 4, 2), AXES)
    spec = P(("zl", "x"), ("y", "zh", "c"))
    return jax.shard_map(
        per_device, mesh=fine, in_specs=(spec,) * 3, out_specs=(spec,) * 3, check_vma=False
    )
```

```python
import functools
import math

import jax
import jax.numpy as jnp
from jax import lax
from jax.experimental import pallas as pl
from jax.experimental.pallas import tpu as pltpu
from jax.sharding import Mesh
from jax.sharding import PartitionSpec as P

slope_coef = math.sqrt(2.0 / math.pi)
AXES = ("zl", "x", "y", "zh", "c")
SIZES = {"zl": 2, "x": 4, "y": 4, "zh": 4, "c": 2}
BF16, F32 = jnp.bfloat16, jnp.float32
MIB = 1024 * 1024
HBM = pl.BlockSpec(memory_space=pl.ANY)
VMEM = pl.BlockSpec(memory_space=pltpu.VMEM)
SMEM = pl.BlockSpec(memory_space=pltpu.SMEM)


def flip(value, axis, mask):
    return lax.ppermute(value, axis, [(i, i ^ mask) for i in range(SIZES[axis])])


def over_z(value):
    return flip(value, "zl", 1)


def over_near(value):
    return flip(value, "y", 1)


def over_far(value):
    return flip(value, "y", 3)


def add_top(block, came):
    n = came.shape[0]
    return jnp.concatenate([added(block[:n], [came]).astype(BF16), block[n:]])


def add_low(block, came):
    n = block.shape[0] - came.shape[0]
    return jnp.concatenate([block[:n], added(block[n:], [came]).astype(BF16)])


def spread_pairs(turn):
    pairs = []
    for zl in range(2):
        for y in range(4):
            to_y = y if y >> 1 == zl ^ turn else y ^ 3
            pairs.append((zl * 4 + y, (y >> 1) * 4 + to_y))
    return pairs


def spread(value, turn):
    return lax.ppermute(value, ("zl", "y"), spread_pairs(turn))


def spread_back(value, turn):
    return lax.ppermute(value, ("zl", "y"), [(b, a) for a, b in spread_pairs(turn)])


def call(kernel, out_shape, in_specs, out_specs, scratch, flops, nbytes, limit):
    return pl.pallas_call(
        kernel,
        out_shape=out_shape,
        in_specs=in_specs,
        out_specs=out_specs,
        scratch_shapes=scratch,
        compiler_params=pltpu.CompilerParams(vmem_limit_bytes=limit),
        cost_estimate=pl.CostEstimate(flops=flops, bytes_accessed=nbytes, transcendentals=0),
    )


def run_copies(copies):
    for copy in copies:
        copy.start()
    for copy in copies:
        copy.wait()


def weight_row(idx, near, dz, dc):
    zl, y, zh, c = idx[0], idx[2], idx[3], idx[4]
    upper = near ^ zl ^ (y & 1) ^ (y >> 1)
    return pl.multiple_of(((upper * 4 + (zh ^ dz)) * 2 + (c ^ dc)) * 192, 192)


def join_kernel(n, *refs):
    *ins, out, sems = refs
    copies = []
    for i, a in enumerate(ins):
        copies.append(pltpu.make_async_copy(a, out.at[pl.ds(i * n, n), :], sems.at[i]))
    run_copies(copies)


def join(*values):
    rows, width = values[0].shape
    return call(
        functools.partial(join_kernel, rows),
        jax.ShapeDtypeStruct((len(values) * rows, width), BF16),
        [HBM] * len(values),
        VMEM,
        [pltpu.SemaphoreType.DMA((len(values),))],
        0,
        4 * len(values) * rows * width,
        8 * MIB,
    )(*values)


def across(a, w):
    return lax.dot_general(a, w, (((0,), (0,)), ((), ())), preferred_element_type=F32)


def turn_of(idx):
    return idx[2] >> 1


def project_kernel(idx, own, other, w, top, low, w0, w1, a_v, w_v, acc, a_sems, w_sems, out_sems):
    loads = [
        pltpu.make_async_copy(a, a_v.at[dc], a_sems.at[dc]) for dc, a in enumerate((own, other))
    ]
    copies = []
    for dc in range(2):
        for near in range(2):
            for dz in range(4):
                copies.append(
                    pltpu.make_async_copy(
                        w.at[pl.ds(weight_row(idx, near, dz, dc), 192), :],
                        w_v.at[dc, pl.ds((near * 4 + dz) * 192, 192), :],
                        w_sems.at[len(copies)],
                    )
                )
    loads[0].start()
    for copy in copies[:8]:
        copy.start()
    loads[1].start()
    for copy in copies[8:]:
        copy.start()
    stores = []
    n = a_v.shape[-1]
    for step in range(4):
        dc, near = step // 2, step % 2
        if near == 0:
            loads[dc].wait()
        for copy in copies[4 * step : 4 * step + 4]:
            copy.wait()
        if near == 1:
            stores.append(pltpu.make_async_copy(w_v.at[dc], (w0, w1)[dc], out_sems.at[dc]))
            stores[-1].start()
        rows = slice(near * 768, near * 768 + 768)
        for half in range(2):
            part = across(a_v[dc, half ^ turn_of(idx), rows], w_v[dc, rows])
            if step > 0:
                part = acc[half] + part
            if step < 3:
                acc[half] = part
            else:
                (top, low)[half][...] = part.astype(BF16)
    for store in stores:
        store.wait()


def project(idx, own, other, w_all):
    width = own.shape[-1]
    return call(
        project_kernel,
        [jax.ShapeDtypeStruct((width, 768), BF16)] * 2
        + [jax.ShapeDtypeStruct((1536, 768), BF16)] * 2,
        [SMEM, HBM, HBM, HBM],
        [VMEM, VMEM, HBM, HBM],
        [
            pltpu.VMEM((2, 2, 1536, width), BF16),
            pltpu.VMEM((2, 1536, 768), BF16),
            pltpu.VMEM((2, width, 768), F32),
            pltpu.SemaphoreType.DMA((2,)),
            pltpu.SemaphoreType.DMA((16,)),
            pltpu.SemaphoreType.DMA((2,)),
        ],
        16 * width * 768 * 768,
        20 << 20,
        58 * MIB,
    )(idx, own.reshape(2, 1536, width), other.reshape(2, 1536, width), w_all)


def half_kernel(idx, a, w, *refs):
    *acc, out = refs
    n = a.shape[-1]
    for half in range(2):
        rows = slice(half * n, half * n + n)
        part = across(a[half ^ turn_of(idx)], w[...])
        out[rows] = acc[0][rows] + part if acc else part


def project_half(idx, a, w, acc):
    width = a.shape[-1]
    return call(
        half_kernel,
        jax.ShapeDtypeStruct((2 * width, 768), F32),
        [SMEM] + [VMEM] * (2 + len(acc)),
        VMEM,
        [],
        8 * width * 768 * 768,
        20 * 1024 * width,
        20 * MIB,
    )(idx, a.reshape(2, 1536, width), w, *acc)


def input_grad_kernel(idx, g, w, out):
    n = out.shape[-1]
    for half in range(2):
        upper = half ^ turn_of(idx)
        part = lax.dot_general(
            w[...],
            g[half * n : half * n + n],
            (((1,), (1,)), ((), ())),
            preferred_element_type=F32,
        ).astype(BF16)
        for near in range(2):
            out[upper * 2 + (near ^ upper)] = part[near * 768 : near * 768 + 768]


def input_grad(idx, g, w):
    width = g.shape[0] // 2
    return call(
        input_grad_kernel,
        jax.ShapeDtypeStruct((4, 768, width), BF16),
        [SMEM] + [VMEM] * 2,
        VMEM,
        [],
        8 * width * 768 * 768,
        20 * 1024 * width,
        20 * MIB,
    )(idx, g, w)


def weight_grad_kernel(idx, g, own, other, *refs):
    *acc, out = refs
    n = own.shape[-1]
    for dc, a in enumerate((own, other)):
        for near in range(2):
            total = None
            for half in range(2):
                term = jnp.dot(
                    a[half ^ turn_of(idx), near * 768 : near * 768 + 768, :],
                    g[half * n : half * n + n],
                    preferred_element_type=F32,
                )
                total = term if total is None else total + term
            for dz in range(4):
                part = total[dz * 192 : dz * 192 + 192]
                rows = pl.ds(weight_row(idx, near, dz, dc), 192)
                if acc:
                    part = part + acc[0][rows, :].astype(F32)
                out[rows, :] = part.astype(BF16)


def weight_grad(idx, g, own, other, acc):
    width = own.shape[-1]
    return call(
        weight_grad_kernel,
        jax.ShapeDtypeStruct((3072, 768), BF16),
        [SMEM] + [VMEM] * (3 + len(acc)),
        VMEM,
        [],
        16 * width * 768 * 768,
        16 << 20,
        24 * MIB,
    )(idx, g, own.reshape(2, 1536, width), other.reshape(2, 1536, width), *acc)


def gelu_pair(pre_act, grad_out):
    inside = slope_coef * (pre_act + 0.044715 * pre_act * pre_act * pre_act)
    tangent = jnp.tanh(inside)
    activated = 0.5 * pre_act * (1.0 + tangent)
    slope = 0.5 * (1.0 + tangent) + 0.5 * pre_act * (1.0 - tangent * tangent) * slope_coef * (
        1.0 + 3.0 * 0.044715 * pre_act * pre_act
    )
    return activated.astype(BF16), (grad_out.astype(F32) * slope).astype(BF16)


def stage(*values):
    return lax.optimization_barrier(values)


def added(first, others):
    total = first.astype(F32)
    for other in others:
        total = total + other.astype(F32)
    return total


def gather_pieces(value, axis):
    return [value] + [flip(value, axis, d) for d in (1, 2, 3)]


def in_order(planes):
    return join(planes[0], planes[1], planes[3], planes[2])


def per_device(tokens, weight, grad_out):
    idx = jnp.stack([lax.axis_index(axis) for axis in AXES]).astype(jnp.int32)
    n = 256
    w_all = lax.all_gather(weight, "x", axis=0, tiled=True)
    zl, upper = idx[0], idx[2] >> 1
    turned = tokens.T
    first, last = turned[:, :n], turned[:, n:]
    came0 = spread(jnp.where(zl == 0, first, last), 0)
    came1 = spread(jnp.where(zl == 0, last, first), 1)
    piece_p = jnp.where(upper == zl, came1, came0)
    piece_o = jnp.where(upper == zl, came0, came1)
    *pieces_p, piece_o = stage(*gather_pieces(piece_p, "zh"), piece_o)

    pieces_o = gather_pieces(piece_o, "zh")
    planes_p = gather_pieces(join(*pieces_p), "y")
    stages = stage(*planes_p, *pieces_o)
    planes_p, pieces_o = stages[:4], stages[4:]

    own_p = in_order(planes_p)
    planes_o = gather_pieces(join(*pieces_o), "y")
    other_p = flip(own_p, "c", 1)
    top, low, w0, w1 = project(idx, own_p, other_p, w_all)
    *planes_o, came_top = stage(*planes_o, over_z(top))
    came_low = over_z(low)

    own_o = in_order(planes_o)
    other_o = flip(own_o, "c", 1)
    pre_act = project_half(idx, other_o, w1, [project_half(idx, own_o, w0, [])])
    came = jnp.concatenate([came_top, came_low])
    activated, grad_o = gelu_pair(added(pre_act, [came]), grad_out)
    grad_p = over_z(grad_o)

    half = flip(input_grad(idx, grad_o, w1), "c", 1)
    both_o = added(input_grad(idx, grad_o, w0), [half]).astype(BF16)
    rows_o = [flip(both_o[d], "y", d) for d in (1, 2, 3)]
    partial = weight_grad(idx, grad_o, own_o, other_o, [])
    grad_p, partial, rows_o[0], rows_o[2] = stage(grad_p, partial, rows_o[0], rows_o[2])

    partial = weight_grad(idx, grad_p, own_p, other_p, [partial])
    partial, grad_p, rows_o[1] = stage(partial, grad_p, rows_o[1])
    grad_weight = lax.psum_scatter(partial, "x", scatter_dimension=0, tiled=True)
    half = flip(input_grad(idx, grad_p, w1), "c", 1)
    both_p = added(input_grad(idx, grad_p, w0), [half]).astype(BF16)
    rows_p = [flip(both_p[d], "y", d) for d in (1, 2, 3)]
    line_o = added(both_o[0], rows_o).astype(BF16).reshape(4, 192, n)
    homes_o = [flip(line_o[d], "zh", d) for d in (1, 2, 3)]
    stages = stage(*rows_p, *homes_o)
    rows_p, homes_o = stages[:3], stages[3:]
    line_p = added(both_p[0], rows_p).astype(BF16).reshape(4, 192, n)
    homes_p = [flip(line_p[d], "zh", d) for d in (1, 2, 3)]
    final_o = added(line_o[0], homes_o).astype(BF16)
    final_p = added(line_p[0], homes_p).astype(BF16)
    back0 = spread_back(jnp.where(upper == zl, final_o, final_p), 0)
    back1 = spread_back(jnp.where(upper == zl, final_p, final_o), 1)
    first = jnp.where(zl == 0, back0, back1)
    last = jnp.where(zl == 0, back1, back0)
    grad_tokens = jnp.concatenate([first, last], axis=1).T
    return activated, grad_tokens, grad_weight


def solution(mesh):
    fine = Mesh(mesh.devices.reshape(2, 4, 4, 4, 2), AXES)
    spec = P(("zl", "x"), ("y", "zh", "c"))
    return jax.shard_map(
        per_device, mesh=fine, in_specs=(spec,) * 3, out_specs=(spec,) * 3, check_vma=False
    )
```

```python
import functools
import math

import jax
import jax.numpy as jnp
from jax import lax
from jax.experimental import pallas as pl
from jax.experimental.pallas import tpu as pltpu
from jax.sharding import Mesh
from jax.sharding import PartitionSpec as P

slope_coef = math.sqrt(2.0 / math.pi)
AXES = ("zl", "x", "y", "zh", "c")
SIZES = {"zl": 2, "x": 4, "y": 4, "zh": 4, "c": 2}
BF16, F32 = jnp.bfloat16, jnp.float32
MIB = 1024 * 1024
HBM = pl.BlockSpec(memory_space=pl.ANY)
VMEM = pl.BlockSpec(memory_space=pltpu.VMEM)
SMEM = pl.BlockSpec(memory_space=pltpu.SMEM)


def flip(value, axis, mask):
    return lax.ppermute(value, axis, [(i, i ^ mask) for i in range(SIZES[axis])])


def over_z(value):
    return flip(value, "zl", 1)


def over_near(value):
    return flip(value, "y", 1)


def over_far(value):
    return flip(value, "y", 3)


def add_top(block, came):
    n = came.shape[0]
    return jnp.concatenate([added(block[:n], [came]).astype(BF16), block[n:]])


def add_low(block, came):
    n = block.shape[0] - came.shape[0]
    return jnp.concatenate([block[:n], added(block[n:], [came]).astype(BF16)])


def spread_pairs(turn):
    pairs = []
    for zl in range(2):
        for y in range(4):
            to_y = y if y >> 1 == zl ^ turn else y ^ 3
            pairs.append((zl * 4 + y, (y >> 1) * 4 + to_y))
    return pairs


def spread(value, turn):
    return lax.ppermute(value, ("zl", "y"), spread_pairs(turn))


def spread_back(value, turn):
    return lax.ppermute(value, ("zl", "y"), [(b, a) for a, b in spread_pairs(turn)])


def call(kernel, out_shape, in_specs, out_specs, scratch, flops, nbytes, limit):
    return pl.pallas_call(
        kernel,
        out_shape=out_shape,
        in_specs=in_specs,
        out_specs=out_specs,
        scratch_shapes=scratch,
        compiler_params=pltpu.CompilerParams(vmem_limit_bytes=limit),
        cost_estimate=pl.CostEstimate(flops=flops, bytes_accessed=nbytes, transcendentals=0),
    )


def run_copies(copies):
    for copy in copies:
        copy.start()
    for copy in copies:
        copy.wait()


def weight_row(idx, near, dz, dc):
    zl, y, zh, c = idx[0], idx[2], idx[3], idx[4]
    upper = near ^ zl ^ (y & 1) ^ (y >> 1)
    return pl.multiple_of(((upper * 4 + (zh ^ dz)) * 2 + (c ^ dc)) * 192, 192)


def join_kernel(n, *refs):
    *ins, out, sems = refs
    copies = []
    for i, a in enumerate(ins):
        copies.append(pltpu.make_async_copy(a, out.at[pl.ds(i * n, n), :], sems.at[i]))
    run_copies(copies)


def join(*values):
    rows, width = values[0].shape
    return call(
        functools.partial(join_kernel, rows),
        jax.ShapeDtypeStruct((len(values) * rows, width), BF16),
        [HBM] * len(values),
        VMEM,
        [pltpu.SemaphoreType.DMA((len(values),))],
        0,
        4 * len(values) * rows * width,
        8 * MIB,
    )(*values)


def across(a, w):
    return lax.dot_general(a, w, (((0,), (0,)), ((), ())), preferred_element_type=F32)


def turn_of(idx):
    return idx[2] >> 1


def project_kernel(idx, own, other, w, top, low, a_v, w_v, acc, a_sems, w_sems):
    loads = [
        pltpu.make_async_copy(a, a_v.at[dc], a_sems.at[dc]) for dc, a in enumerate((own, other))
    ]
    copies = []
    for dc in range(2):
        for near in range(2):
            for dz in range(4):
                copies.append(
                    pltpu.make_async_copy(
                        w.at[pl.ds(weight_row(idx, near, dz, dc), 192), :],
                        w_v.at[dc, pl.ds((near * 4 + dz) * 192, 192), :],
                        w_sems.at[len(copies)],
                    )
                )
    loads[0].start()
    for copy in copies[:8]:
        copy.start()
    loads[1].start()
    for copy in copies[8:]:
        copy.start()
    n = a_v.shape[-1]
    for step in range(4):
        dc, near = step // 2, step % 2
        if near == 0:
            loads[dc].wait()
        for copy in copies[4 * step : 4 * step + 4]:
            copy.wait()
        rows = slice(near * 768, near * 768 + 768)
        for half in range(2):
            part = across(a_v[dc, half ^ turn_of(idx), rows], w_v[dc, rows])
            if step > 0:
                part = acc[half] + part
            if step < 3:
                acc[half] = part
            else:
                (top, low)[half][...] = part.astype(BF16)


def project(idx, own, other, w_all):
    width = own.shape[-1]
    return call(
        project_kernel,
        [jax.ShapeDtypeStruct((width, 768), BF16)] * 2,
        [SMEM, HBM, HBM, HBM],
        [VMEM, VMEM],
        [
            pltpu.VMEM((2, 2, 1536, width), BF16),
            pltpu.VMEM((2, 1536, 768), BF16),
            pltpu.VMEM((2, width, 768), F32),
            pltpu.SemaphoreType.DMA((2,)),
            pltpu.SemaphoreType.DMA((16,)),
        ],
        16 * width * 768 * 768,
        20 << 20,
        58 * MIB,
    )(idx, own.reshape(2, 1536, width), other.reshape(2, 1536, width), w_all)


def arrange_kernel(idx, w, w0, w1, sems):
    copies = []
    for dc, out in enumerate((w0, w1)):
        for near in range(2):
            for dz in range(4):
                copies.append(
                    pltpu.make_async_copy(
                        w.at[pl.ds(weight_row(idx, near, dz, dc), 192), :],
                        out.at[pl.ds((near * 4 + dz) * 192, 192), :],
                        sems.at[len(copies)],
                    )
                )
    run_copies(copies)


def arrange(idx, w):
    return call(
        arrange_kernel,
        [jax.ShapeDtypeStruct((1536, 768), BF16)] * 2,
        [SMEM, HBM],
        [VMEM] * 2,
        [pltpu.SemaphoreType.DMA((16,))],
        0,
        10 << 20,
        12 * MIB,
    )(idx, w)


def half_kernel(idx, a, w, *refs):
    *acc, out = refs
    n = a.shape[-1]
    for half in range(2):
        rows = slice(half * n, half * n + n)
        part = across(a[half ^ turn_of(idx)], w[...])
        out[rows] = acc[0][rows] + part if acc else part


def project_half(idx, a, w, acc):
    width = a.shape[-1]
    return call(
        half_kernel,
        jax.ShapeDtypeStruct((2 * width, 768), F32),
        [SMEM] + [VMEM] * (2 + len(acc)),
        VMEM,
        [],
        8 * width * 768 * 768,
        20 * 1024 * width,
        20 * MIB,
    )(idx, a.reshape(2, 1536, width), w, *acc)


def input_grad_kernel(idx, g, w, out):
    n = out.shape[-1]
    for half in range(2):
        upper = half ^ turn_of(idx)
        part = lax.dot_general(
            w[...],
            g[half * n : half * n + n],
            (((1,), (1,)), ((), ())),
            preferred_element_type=F32,
        ).astype(BF16)
        for near in range(2):
            out[upper * 2 + (near ^ upper)] = part[near * 768 : near * 768 + 768]


def input_grad(idx, g, w):
    width = g.shape[0] // 2
    return call(
        input_grad_kernel,
        jax.ShapeDtypeStruct((4, 768, width), BF16),
        [SMEM] + [VMEM] * 2,
        VMEM,
        [],
        8 * width * 768 * 768,
        20 * 1024 * width,
        20 * MIB,
    )(idx, g, w)


def weight_grad_kernel(idx, g, own, other, *refs):
    *acc, out = refs
    n = own.shape[-1]
    for dc, a in enumerate((own, other)):
        for near in range(2):
            total = None
            for half in range(2):
                term = jnp.dot(
                    a[half ^ turn_of(idx), near * 768 : near * 768 + 768, :],
                    g[half * n : half * n + n],
                    preferred_element_type=F32,
                )
                total = term if total is None else total + term
            for dz in range(4):
                part = total[dz * 192 : dz * 192 + 192]
                rows = pl.ds(weight_row(idx, near, dz, dc), 192)
                if acc:
                    part = part + acc[0][rows, :].astype(F32)
                out[rows, :] = part.astype(BF16)


def weight_grad(idx, g, own, other, acc):
    width = own.shape[-1]
    return call(
        weight_grad_kernel,
        jax.ShapeDtypeStruct((3072, 768), BF16),
        [SMEM] + [VMEM] * (3 + len(acc)),
        VMEM,
        [],
        16 * width * 768 * 768,
        16 << 20,
        24 * MIB,
    )(idx, g, own.reshape(2, 1536, width), other.reshape(2, 1536, width), *acc)


def gelu_pair(pre_act, grad_out):
    inside = slope_coef * (pre_act + 0.044715 * pre_act * pre_act * pre_act)
    tangent = jnp.tanh(inside)
    activated = 0.5 * pre_act * (1.0 + tangent)
    slope = 0.5 * (1.0 + tangent) + 0.5 * pre_act * (1.0 - tangent * tangent) * slope_coef * (
        1.0 + 3.0 * 0.044715 * pre_act * pre_act
    )
    return activated.astype(BF16), (grad_out.astype(F32) * slope).astype(BF16)


def stage(*values):
    return lax.optimization_barrier(values)


def added(first, others):
    total = first.astype(F32)
    for other in others:
        total = total + other.astype(F32)
    return total


def gather_pieces(value, axis):
    return [value] + [flip(value, axis, d) for d in (1, 2, 3)]


def in_order(planes):
    return join(planes[0], planes[1], planes[3], planes[2])


def per_device(tokens, weight, grad_out):
    idx = jnp.stack([lax.axis_index(axis) for axis in AXES]).astype(jnp.int32)
    n = 256
    w_all = lax.all_gather(weight, "x", axis=0, tiled=True)
    zl, upper = idx[0], idx[2] >> 1
    turned = tokens.T
    first, last = turned[:, :n], turned[:, n:]
    came0 = spread(jnp.where(zl == 0, first, last), 0)
    came1 = spread(jnp.where(zl == 0, last, first), 1)
    piece_p = jnp.where(upper == zl, came1, came0)
    piece_o = jnp.where(upper == zl, came0, came1)
    *pieces_p, piece_o = stage(*gather_pieces(piece_p, "zh"), piece_o)

    pieces_o = gather_pieces(piece_o, "zh")
    planes_p = gather_pieces(join(*pieces_p), "y")
    stages = stage(*planes_p, *pieces_o)
    planes_p, pieces_o = stages[:4], stages[4:]

    own_p = in_order(planes_p)
    planes_o = gather_pieces(join(*pieces_o), "y")
    other_p = flip(own_p, "c", 1)
    top, low = project(idx, own_p, other_p, w_all)
    w_all, top = stage(w_all, top)
    w0, w1 = arrange(idx, w_all)
    came_low = over_z(low)

    own_o, came_top = stage(in_order(planes_o), over_z(top))
    other_o = flip(own_o, "c", 1)
    pre_act = project_half(idx, other_o, w1, [project_half(idx, own_o, w0, [])])
    came = jnp.concatenate([came_top, came_low])
    activated, grad_o = gelu_pair(added(pre_act, [came]), grad_out)
    grad_p = over_z(grad_o)

    half = flip(input_grad(idx, grad_o, w1), "c", 1)
    both_o = added(input_grad(idx, grad_o, w0), [half]).astype(BF16)
    rows_o = [flip(both_o[d], "y", d) for d in (1, 2, 3)]
    partial = weight_grad(idx, grad_o, own_o, other_o, [])
    grad_p, partial, rows_o[0], rows_o[2] = stage(grad_p, partial, rows_o[0], rows_o[2])

    partial = weight_grad(idx, grad_p, own_p, other_p, [partial])
    partial, grad_p, rows_o[1] = stage(partial, grad_p, rows_o[1])
    grad_weight = lax.psum_scatter(partial, "x", scatter_dimension=0, tiled=True)
    half = flip(input_grad(idx, grad_p, w1), "c", 1)
    both_p = added(input_grad(idx, grad_p, w0), [half]).astype(BF16)
    rows_p = [flip(both_p[d], "y", d) for d in (1, 2, 3)]
    line_o = added(both_o[0], rows_o).astype(BF16).reshape(4, 192, n)
    homes_o = [flip(line_o[d], "zh", d) for d in (1, 2, 3)]
    stages = stage(*rows_p, *homes_o)
    rows_p, homes_o = stages[:3], stages[3:]
    line_p = added(both_p[0], rows_p).astype(BF16).reshape(4, 192, n)
    homes_p = [flip(line_p[d], "zh", d) for d in (1, 2, 3)]
    final_o = added(line_o[0], homes_o).astype(BF16)
    final_p = added(line_p[0], homes_p).astype(BF16)
    back0 = spread_back(jnp.where(upper == zl, final_o, final_p), 0)
    back1 = spread_back(jnp.where(upper == zl, final_p, final_o), 1)
    first = jnp.where(zl == 0, back0, back1)
    last = jnp.where(zl == 0, back1, back0)
    grad_tokens = jnp.concatenate([first, last], axis=1).T
    return activated, grad_tokens, grad_weight


def solution(mesh):
    fine = Mesh(mesh.devices.reshape(2, 4, 4, 4, 2), AXES)
    spec = P(("zl", "x"), ("y", "zh", "c"))
    return jax.shard_map(
        per_device, mesh=fine, in_specs=(spec,) * 3, out_specs=(spec,) * 3, check_vma=False
    )
```

```python
import functools
import math

import jax
import jax.numpy as jnp
from jax import lax
from jax.experimental import pallas as pl
from jax.experimental.pallas import tpu as pltpu
from jax.sharding import Mesh
from jax.sharding import PartitionSpec as P

slope_coef = math.sqrt(2.0 / math.pi)
AXES = ("zl", "x", "y", "zh", "c")
SIZES = {"zl": 2, "x": 4, "y": 4, "zh": 4, "c": 2}
BF16, F32 = jnp.bfloat16, jnp.float32
MIB = 1024 * 1024
HBM = pl.BlockSpec(memory_space=pl.ANY)
VMEM = pl.BlockSpec(memory_space=pltpu.VMEM)
SMEM = pl.BlockSpec(memory_space=pltpu.SMEM)


def flip(value, axis, mask):
    return lax.ppermute(value, axis, [(i, i ^ mask) for i in range(SIZES[axis])])


def over_z(value):
    return flip(value, "zl", 1)


def over_near(value):
    return flip(value, "y", 1)


def over_far(value):
    return flip(value, "y", 3)


def add_top(block, came):
    n = came.shape[0]
    return jnp.concatenate([added(block[:n], [came]).astype(BF16), block[n:]])


def add_low(block, came):
    n = block.shape[0] - came.shape[0]
    return jnp.concatenate([block[:n], added(block[n:], [came]).astype(BF16)])


def spread_pairs(turn):
    pairs = []
    for zl in range(2):
        for y in range(4):
            to_y = y if y >> 1 == zl ^ turn else y ^ 3
            pairs.append((zl * 4 + y, (y >> 1) * 4 + to_y))
    return pairs


def spread(value, turn):
    return lax.ppermute(value, ("zl", "y"), spread_pairs(turn))


def spread_back(value, turn):
    return lax.ppermute(value, ("zl", "y"), [(b, a) for a, b in spread_pairs(turn)])


def call(kernel, out_shape, in_specs, out_specs, scratch, flops, nbytes, limit):
    return pl.pallas_call(
        kernel,
        out_shape=out_shape,
        in_specs=in_specs,
        out_specs=out_specs,
        scratch_shapes=scratch,
        compiler_params=pltpu.CompilerParams(vmem_limit_bytes=limit),
        cost_estimate=pl.CostEstimate(flops=flops, bytes_accessed=nbytes, transcendentals=0),
    )


def run_copies(copies):
    for copy in copies:
        copy.start()
    for copy in copies:
        copy.wait()


def weight_row(idx, near, dz, dc):
    zl, y, zh, c = idx[0], idx[2], idx[3], idx[4]
    upper = near ^ zl ^ (y & 1) ^ (y >> 1)
    return pl.multiple_of(((upper * 4 + (zh ^ dz)) * 2 + (c ^ dc)) * 192, 192)


def join_kernel(n, *refs):
    *ins, out, sems = refs
    copies = []
    for i, a in enumerate(ins):
        copies.append(pltpu.make_async_copy(a, out.at[pl.ds(i * n, n), :], sems.at[i]))
    run_copies(copies)


def join(*values):
    rows, width = values[0].shape
    return call(
        functools.partial(join_kernel, rows),
        jax.ShapeDtypeStruct((len(values) * rows, width), BF16),
        [HBM] * len(values),
        VMEM,
        [pltpu.SemaphoreType.DMA((len(values),))],
        0,
        4 * len(values) * rows * width,
        8 * MIB,
    )(*values)


def across(a, w):
    return lax.dot_general(a, w, (((0,), (0,)), ((), ())), preferred_element_type=F32)


def turn_of(idx):
    return idx[2] >> 1


def project_kernel(idx, own, other, w, top, low, a_v, w_v, acc, a_sems, w_sems):
    loads = [
        pltpu.make_async_copy(a, a_v.at[dc], a_sems.at[dc]) for dc, a in enumerate((own, other))
    ]
    copies = []
    for dc in range(2):
        for near in range(2):
            for dz in range(4):
                copies.append(
                    pltpu.make_async_copy(
                        w.at[pl.ds(weight_row(idx, near, dz, dc), 192), :],
                        w_v.at[dc, pl.ds((near * 4 + dz) * 192, 192), :],
                        w_sems.at[len(copies)],
                    )
                )
    loads[0].start()
    for copy in copies[:8]:
        copy.start()
    loads[1].start()
    for copy in copies[8:]:
        copy.start()
    n = a_v.shape[-1]
    for step in range(4):
        dc, near = step // 2, step % 2
        if near == 0:
            loads[dc].wait()
        for copy in copies[4 * step : 4 * step + 4]:
            copy.wait()
        rows = slice(near * 768, near * 768 + 768)
        for half in range(2):
            part = across(a_v[dc, half ^ turn_of(idx), rows], w_v[dc, rows])
            if step > 0:
                part = acc[half] + part
            if step < 3:
                acc[half] = part
            else:
                (top, low)[half][...] = part.astype(BF16)


def project(idx, own, other, w_all):
    width = own.shape[-1]
    return call(
        project_kernel,
        [jax.ShapeDtypeStruct((width, 768), BF16)] * 2,
        [SMEM, HBM, HBM, HBM],
        [VMEM, VMEM],
        [
            pltpu.VMEM((2, 2, 1536, width), BF16),
            pltpu.VMEM((2, 1536, 768), BF16),
            pltpu.VMEM((2, width, 768), F32),
            pltpu.SemaphoreType.DMA((2,)),
            pltpu.SemaphoreType.DMA((16,)),
        ],
        16 * width * 768 * 768,
        20 << 20,
        58 * MIB,
    )(idx, own.reshape(2, 1536, width), other.reshape(2, 1536, width), w_all)


def arrange_kernel(idx, w, w0, w1, sems):
    copies = []
    for dc, out in enumerate((w0, w1)):
        for near in range(2):
            for dz in range(4):
                copies.append(
                    pltpu.make_async_copy(
                        w.at[pl.ds(weight_row(idx, near, dz, dc), 192), :],
                        out.at[pl.ds((near * 4 + dz) * 192, 192), :],
                        sems.at[len(copies)],
                    )
                )
    run_copies(copies)


def arrange(idx, w):
    return call(
        arrange_kernel,
        [jax.ShapeDtypeStruct((1536, 768), BF16)] * 2,
        [SMEM, HBM],
        [VMEM] * 2,
        [pltpu.SemaphoreType.DMA((16,))],
        0,
        10 << 20,
        12 * MIB,
    )(idx, w)


def half_kernel(idx, a, w, *refs):
    *acc, out = refs
    n = a.shape[-1]
    for half in range(2):
        rows = slice(half * n, half * n + n)
        part = across(a[half ^ turn_of(idx)], w[...])
        out[rows] = acc[0][rows] + part if acc else part


def project_half(idx, a, w, acc):
    width = a.shape[-1]
    return call(
        half_kernel,
        jax.ShapeDtypeStruct((2 * width, 768), F32),
        [SMEM] + [VMEM] * (2 + len(acc)),
        VMEM,
        [],
        8 * width * 768 * 768,
        20 * 1024 * width,
        20 * MIB,
    )(idx, a.reshape(2, 1536, width), w, *acc)


def input_grad_kernel(idx, g, w, out):
    n = out.shape[-1]
    for half in range(2):
        upper = half ^ turn_of(idx)
        part = lax.dot_general(
            w[...],
            g[half * n : half * n + n],
            (((1,), (1,)), ((), ())),
            preferred_element_type=F32,
        ).astype(BF16)
        for near in range(2):
            out[upper * 2 + (near ^ upper)] = part[near * 768 : near * 768 + 768]


def input_grad(idx, g, w):
    width = g.shape[0] // 2
    return call(
        input_grad_kernel,
        jax.ShapeDtypeStruct((4, 768, width), BF16),
        [SMEM] + [VMEM] * 2,
        VMEM,
        [],
        8 * width * 768 * 768,
        20 * 1024 * width,
        20 * MIB,
    )(idx, g, w)


def weight_grad_kernel(idx, g, own, other, *refs):
    *acc, out = refs
    n = own.shape[-1]
    for dc, a in enumerate((own, other)):
        for near in range(2):
            total = None
            for half in range(2):
                term = jnp.dot(
                    a[half ^ turn_of(idx), near * 768 : near * 768 + 768, :],
                    g[half * n : half * n + n],
                    preferred_element_type=F32,
                )
                total = term if total is None else total + term
            for dz in range(4):
                part = total[dz * 192 : dz * 192 + 192]
                rows = pl.ds(weight_row(idx, near, dz, dc), 192)
                if acc:
                    part = part + acc[0][rows, :].astype(F32)
                out[rows, :] = part.astype(BF16)


def weight_grad(idx, g, own, other, acc):
    width = own.shape[-1]
    return call(
        weight_grad_kernel,
        jax.ShapeDtypeStruct((3072, 768), BF16),
        [SMEM] + [VMEM] * (3 + len(acc)),
        VMEM,
        [],
        16 * width * 768 * 768,
        16 << 20,
        24 * MIB,
    )(idx, g, own.reshape(2, 1536, width), other.reshape(2, 1536, width), *acc)


def gelu_pair(pre_act, grad_out):
    inside = slope_coef * (pre_act + 0.044715 * pre_act * pre_act * pre_act)
    tangent = jnp.tanh(inside)
    activated = 0.5 * pre_act * (1.0 + tangent)
    slope = 0.5 * (1.0 + tangent) + 0.5 * pre_act * (1.0 - tangent * tangent) * slope_coef * (
        1.0 + 3.0 * 0.044715 * pre_act * pre_act
    )
    return activated.astype(BF16), (grad_out.astype(F32) * slope).astype(BF16)


def stage(*values):
    return lax.optimization_barrier(values)


def added(first, others):
    total = first.astype(F32)
    for other in others:
        total = total + other.astype(F32)
    return total


def gather_pieces(value, axis):
    return [value] + [flip(value, axis, d) for d in (1, 2, 3)]


def in_order(planes):
    return join(planes[0], planes[1], planes[3], planes[2])


def per_device(tokens, weight, grad_out):
    idx = jnp.stack([lax.axis_index(axis) for axis in AXES]).astype(jnp.int32)
    n = 256
    w_all = lax.all_gather(weight, "x", axis=0, tiled=True)
    zl, upper = idx[0], idx[2] >> 1
    turned = tokens.T
    first, last = turned[:, :n], turned[:, n:]
    came0 = spread(jnp.where(zl == 0, first, last), 0)
    came1 = spread(jnp.where(zl == 0, last, first), 1)
    piece_p = jnp.where(upper == zl, came1, came0)
    piece_o = jnp.where(upper == zl, came0, came1)
    *pieces_p, piece_o = stage(*gather_pieces(piece_p, "zh"), piece_o)

    pieces_o = gather_pieces(piece_o, "zh")
    planes_p = gather_pieces(join(*pieces_p), "y")
    stages = stage(*planes_p, *pieces_o)
    planes_p, pieces_o = stages[:4], stages[4:]

    own_p = in_order(planes_p)
    planes_o = gather_pieces(join(*pieces_o), "y")
    other_p = flip(own_p, "c", 1)
    top, low = project(idx, own_p, other_p, w_all)
    w_all, top = stage(w_all, top)
    w0, w1 = arrange(idx, w_all)
    *planes_o, came_top = stage(*planes_o, over_z(top))
    came_low = over_z(low)

    own_o = in_order(planes_o)
    other_o = flip(own_o, "c", 1)
    pre_act = project_half(idx, other_o, w1, [project_half(idx, own_o, w0, [])])
    came = jnp.concatenate([came_top, came_low])
    activated, grad_o = gelu_pair(added(pre_act, [came]), grad_out)
    grad_p = over_z(grad_o)

    half = flip(input_grad(idx, grad_o, w1), "c", 1)
    both_o = added(input_grad(idx, grad_o, w0), [half]).astype(BF16)
    rows_o = [flip(both_o[d], "y", d) for d in (1, 2, 3)]
    partial = weight_grad(idx, grad_o, own_o, other_o, [])
    grad_p, partial, rows_o[0], rows_o[2] = stage(grad_p, partial, rows_o[0], rows_o[2])

    partial = weight_grad(idx, grad_p, own_p, other_p, [partial])
    partial, grad_p, rows_o[1] = stage(partial, grad_p, rows_o[1])
    grad_weight = lax.psum_scatter(partial, "x", scatter_dimension=0, tiled=True)
    half = flip(input_grad(idx, grad_p, w1), "c", 1)
    both_p = added(input_grad(idx, grad_p, w0), [half]).astype(BF16)
    rows_p = [flip(both_p[d], "y", d) for d in (1, 2, 3)]
    line_o = added(both_o[0], rows_o).astype(BF16).reshape(4, 192, n)
    homes_o = [flip(line_o[d], "zh", d) for d in (1, 2, 3)]
    stages = stage(*rows_p, *homes_o)
    rows_p, homes_o = stages[:3], stages[3:]
    line_p = added(both_p[0], rows_p).astype(BF16).reshape(4, 192, n)
    homes_p = [flip(line_p[d], "zh", d) for d in (1, 2, 3)]
    final_o = added(line_o[0], homes_o).astype(BF16)
    final_p = added(line_p[0], homes_p).astype(BF16)
    back0 = spread_back(jnp.where(upper == zl, final_o, final_p), 0)
    back1 = spread_back(jnp.where(upper == zl, final_p, final_o), 1)
    first = jnp.where(zl == 0, back0, back1)
    last = jnp.where(zl == 0, back1, back0)
    grad_tokens = jnp.concatenate([first, last], axis=1).T
    return activated, grad_tokens, grad_weight


def solution(mesh):
    fine = Mesh(mesh.devices.reshape(2, 4, 4, 4, 2), AXES)
    spec = P(("zl", "x"), ("y", "zh", "c"))
    return jax.shard_map(
        per_device, mesh=fine, in_specs=(spec,) * 3, out_specs=(spec,) * 3, check_vma=False
    )
```
